512 devices in a mesh: grp: 16 (over x, y_lo, core), scen: 32 (over y_hi, z).
Axes of the slice: x: 4, y: 4 (y_hi: 2, y_lo: 2; y = y_hi * 2 + y_lo), z: 16, core: 2. Of those that a mesh axis runs over, the one named last changes fastest.
Arguments:
- factors: bfloat16 [512, 1024, 1024], P(('grp', 'scen')), may hold values from -0.1875 to 0.1875
- border: bfloat16 [512, 1024, 1024], P(('grp', 'scen')), may hold values from -24 to 24
- pattern: int32 [512, 8], P(('grp', 'scen')), may hold values 0 or 1
- rhs_second: bfloat16 [512, 1024], P(('grp', 'scen')), may hold values from -6 to 6
- coupling: float32 [1024, 1024], P('scen'), may hold values from -6 to 6
- rhs_first: float32 [1024], replicated, may hold values from -6 to 6
Outputs:
- schur: float32 [1024, 1024], P('scen')
- reduced_rhs: float32 [1024], replicated
The draws below stay inside these ranges and needn't reach their ends.
All inputs are finite; a program needn't handle non-finite values. No bound on the sum of `pattern` on one device may be relied on, other than what follows from the above.
Results may differ from the reference program's by a relative error of at most 0.0024.
Values sent between devices are 32-bit elements; how exact they have to be, the bound alone decides.
No kernel may reach another device: no remote copies, remote signals or barrier semaphores. Data moves between devices by JAX's collectives and lax.ppermute only.
A program may use at most 64 MiB of HBM per device.

```python
import jax
import jax.numpy as jnp
from jax import lax

NS = 1024
N0 = 1024
NB = 8
SCENARIOS = 512


def set_ends(array, key, smallest, high):
    longest = array.shape.index(max(array.shape))
    spots = []
    for shift in (0, 1):
        where = [jax.random.randint(jax.random.fold_in(key, axis), (), 0, length) for axis, length in enumerate(array.shape)]
        where[longest] = (where[longest] + shift) % array.shape[longest]
        spots.append(tuple(where))
    return array.at[spots[0]].set(smallest).at[spots[1]].set(high)


def raised(drawn, own_key, source, target, blocks, factor):
    owner, partner = [(jnp.arange(drawn.shape[axis_at]) // (drawn.shape[axis_at] // blocks)).reshape([-1 if axis == axis_at else 1 for axis in range(drawn.ndim)]) for axis_at in (source, target)]
    chosen = jax.random.permutation(own_key, blocks)[partner]
    strong = (owner == chosen) | (owner == (partner + blocks // 2) % blocks)
    return jnp.where(strong, factor * drawn, drawn)


def steps_of(key, shape, cuts, low, top_value):
    factor_of = 1.0
    for dim, blocks in cuts:
        steps = jax.random.uniform(jax.random.fold_in(jax.random.fold_in(key, 6), dim), (blocks,), jnp.float32, low / len(cuts), top_value / len(cuts))
        factor_of = factor_of * jnp.repeat(jnp.exp(steps), shape[dim] // blocks).reshape((-1,) + (1,) * (len(shape) - 1 - dim))
    return factor_of


def normal_values(stream_key, dims, deviation, reach, pieces=(), kind=jnp.bfloat16):
    values = deviation * jax.random.normal(stream_key, dims, jnp.float32)
    if pieces:
        values = values * steps_of(stream_key, dims, pieces, -0.22, 0.18)
    return jnp.clip(values, -reach, reach).astype(kind)


def bell_draw_with(own_key, shape, spread, reach, cuts, heavy, held_as=jnp.bfloat16):
    result = spread * jax.random.normal(own_key, shape, jnp.float32)
    if cuts:
        result = result * steps_of(own_key, shape, cuts, -0.22, 0.18)
    return jnp.clip(raised(result, jax.random.fold_in(own_key, 3), *heavy), -reach, reach).astype(held_as)


def setup_inputs(seed: int = 0) -> dict:
    seeds = jax.random.split(jax.random.key(seed), 7)
    return {
        "factors": normal_values(seeds[0], (SCENARIOS, NS, NS), NS ** -0.5, 0.1875, ((0, 512),)),
        "border": bell_draw_with(seeds[1], (SCENARIOS, NS, N0), 1.0, 24.0, ((0, 512),), (0, 2, 512, 6.0)),
        "pattern": set_ends((jax.random.randint(seeds[2], (SCENARIOS, NB), 0, 4) < 3).astype(jnp.int32), jax.random.fold_in(seeds[2], 1), 0, 1),
        "rhs_second": normal_values(seeds[3], (SCENARIOS, NS), 1.0, 6.0, ((0, 512),)),
        "coupling": normal_values(seeds[4], (N0, N0), 1.0, 6.0, ((0, 32),), jnp.float32),
        "rhs_first": normal_values(seeds[5], (N0,), 1.0, 6.0, (), jnp.float32),
    }


def reference(factors, border, pattern, rhs_second, coupling, rhs_first):

    def step(carry, items):
        total, carried = carry
        factor, block, marks, second = items
        widen = jnp.repeat(marks, 128).astype(jnp.bfloat16)
        masked = block * widen[None, :]
        linked = jnp.dot(factor, masked, preferred_element_type=jnp.float32).astype(jnp.bfloat16)
        local = jnp.dot(factor, second, preferred_element_type=jnp.float32).astype(jnp.bfloat16)
        total = total + jnp.dot(linked.T, linked, preferred_element_type=jnp.float32)
        carried = carried + jnp.dot(local, linked, preferred_element_type=jnp.float32)
        return ((total, carried), None)
    start = (jnp.zeros((N0, N0), jnp.float32), jnp.zeros((N0,), jnp.float32))
    (total, carried), _ = lax.scan(step, start, (factors, border, pattern, rhs_second))
    schur = coupling - total / (NS * jnp.sqrt(jnp.float32(SCENARIOS)))
    reduced_rhs = rhs_first - carried / jnp.sqrt(jnp.float32(NS * SCENARIOS))
    return (schur, reduced_rhs)
```

```python
import functools
import math

import jax
import jax.numpy as jnp
from jax import lax
from jax.experimental import pallas as pl
from jax.experimental.pallas import tpu as pltpu
from jax.sharding import Mesh
from jax.sharding import PartitionSpec as P

EDGE = 128
BLOCKS = 8
STRIPS = 32
KEPT = 5
STEPS = 4


def gram_kernel(factor, border, marks, second, keep, send, linked, packed, carried):
    step = pl.program_id(0)
    rows = factor.shape[1]
    part = factor[0]
    mask = jnp.concatenate(
        [jnp.full((1, EDGE), marks[0, b].astype(jnp.float32)) for b in range(BLOCKS)], axis=1
    )
    product = jnp.dot(part, border[0], preferred_element_type=jnp.float32) * mask
    rounded = product.astype(jnp.bfloat16)
    linked[pl.ds(pl.multiple_of(step * rows, rows), rows), :] = rounded
    local = jnp.sum(
        part.astype(jnp.float32) * second[...].astype(jnp.float32), axis=1, keepdims=True
    ).astype(jnp.bfloat16)
    term = jnp.sum(local.astype(jnp.float32) * rounded.astype(jnp.float32), axis=0, keepdims=True)

    @pl.when(step == 0)
    def _():
        carried[...] = term

    @pl.when(step > 0)
    def _():
        carried[...] += term

    @pl.when(step == STEPS - 1)
    def _():
        def times(left, right):
            return lax.dot_general(
                left, right, (((0,), (0,)), ((), ())), preferred_element_type=jnp.float32
            )

        for i in range(BLOCKS):
            left = linked[:, i * EDGE : (i + 1) * EDGE]
            count = KEPT if i < BLOCKS // 2 else KEPT - 1
            first = min(count, BLOCKS - i)
            block = times(left, linked[:, i * EDGE : (i + first) * EDGE])
            for d in range(first):
                packed[d, i * EDGE : (i + 1) * EDGE, :] = block[:, d * EDGE : (d + 1) * EDGE]
            if first < count:
                block = times(left, linked[:, : (count - first) * EDGE])
                for d in range(count - first):
                    packed[first + d, i * EDGE : (i + 1) * EDGE, :] = block[
                        :, d * EDGE : (d + 1) * EDGE
                    ]
        half = BLOCKS // 2 * EDGE
        packed[KEPT - 1, half:, :] = jnp.zeros((half, EDGE), jnp.float32)
        for b in range(BLOCKS):
            packed[KEPT - 1, half + b : half + b + 1, :] = carried[:, b * EDGE : (b + 1) * EDGE]
        core = lax.axis_index("core")
        pieces = keep.shape[0]
        for out, side in ((keep, core), (send, 1 - core)):
            for j in range(pieces):
                for d in range(KEPT):
                    out[j, :, d * EDGE : (d + 1) * EDGE] = packed[
                        d, pl.ds(side * pieces + j, STRIPS, stride=STRIPS), :
                    ]


def expand_kernel(arrived, out):
    total = arrived[0]
    for k in range(1, arrived.shape[0]):
        total = total + arrived[k]
    levels = 16
    height = 24
    row = lax.broadcasted_iota(jnp.int32, (STRIPS, EDGE), 0)
    lane = lax.broadcasted_iota(jnp.int32, (STRIPS, EDGE), 1)
    apart = row % 4 - lane // 32

    def put(slot, value):
        out[pl.ds(slot, levels, stride=height), :] = value

    for d in range(KEPT):
        given = total[:, d * EDGE : (d + 1) * EDGE]
        put(d, given[:levels])
        if d < KEPT - 1:
            put(8 + d, given[levels:])
        if d == 0:
            continue
        turned = given
        for k in range(-3, 4):
            if k == 0:
                continue
            moved = pltpu.roll(pltpu.roll(given, k % STRIPS, 0), (-32 * k) % EDGE, 1)
            turned = jnp.where(apart == k, moved, turned)
        if d == KEPT - 1:
            put(8 + 4, turned[:levels])
        else:
            turned = pltpu.roll(turned, 4 * d, 0)
            put(8 - d, turned[:levels])
            put(16 - d, turned[levels:])
    extra = total[levels : levels + 1, (KEPT - 1) * EDGE :]
    put(16, jnp.broadcast_to(extra, (levels, EDGE)))
    for slot in range(17, height):
        put(slot, jnp.zeros((levels, EDGE), jnp.float32))


def spread_kernel(arrived, out):
    total = arrived[0]
    for k in range(1, arrived.shape[0]):
        total = total + arrived[k]
    for j in range(STRIPS):
        out[j, :8, :] = total[8 * (j % 2) : 8 * (j % 2) + 8]
        out[j, 8:, :] = total[16:]


def finish_kernel(arrived, coupling, first, schur, reduced, *, scale, root):
    high, z = lax.axis_index("yhi"), lax.axis_index("z")
    own = high * 4 + z // 4
    height = 16
    slots = [arrived[pl.ds(slot, STRIPS, stride=height), :] for slot in range(8)]
    flipped = jnp.transpose(jnp.concatenate(slots[4:], axis=0))
    for slot in range(8):
        value = slots[slot]
        if slot >= 4:
            at = (slot - 4) * STRIPS
            mirrored = jnp.concatenate(
                [flipped[32 * q : 32 * q + 32, at : at + STRIPS] for q in range(4)], axis=1
            )
            value = mirrored if slot > 4 else jnp.where(high == 0, value, mirrored)
        where = pl.ds(pl.multiple_of(lax.rem(own + slot, 8) * EDGE, EDGE), EDGE)
        schur[:, where] = coupling[:, where] - value / jnp.float32(scale)
    reduced[...] = first[...] - arrived[pl.ds(8, 8, stride=height), :] / jnp.float32(root)


def on_device(factors, border, pattern, rhs_second, coupling, rhs_first):
    _, order, width = factors.shape
    scenarios = 512
    params = functools.partial(pltpu.CompilerParams, vmem_limit_bytes=48 * 1024 * 1024)
    rows = order // STEPS
    half = jax.ShapeDtypeStruct((16, STRIPS, KEPT * EDGE), jnp.float32)
    with jax.named_scope("gram"):
        keep, send = pl.pallas_call(
            gram_kernel,
            grid=(STEPS,),
            out_shape=(half, half),
            in_specs=[
                pl.BlockSpec((1, rows, width), lambda i: (0, i, 0)),
                pl.BlockSpec((1, width, width), lambda i: (0, 0, 0)),
                pl.BlockSpec(memory_space=pltpu.SMEM),
                pl.BlockSpec((1, width), lambda i: (0, 0)),
            ],
            out_specs=(
                pl.BlockSpec(half.shape, lambda i: (0, 0, 0)),
                pl.BlockSpec(half.shape, lambda i: (0, 0, 0)),
            ),
            scratch_shapes=[
                pltpu.VMEM((order, width), jnp.bfloat16),
                pltpu.VMEM((KEPT, order, EDGE), jnp.float32),
                pltpu.VMEM((1, width), jnp.float32),
            ],
            compiler_params=params(),
        )(factors, border, pattern, rhs_second)
    with jax.named_scope("cores"):
        both = keep + lax.ppermute(send, "core", [(0, 1), (1, 0)])
    whole = pl.BlockSpec(memory_space=pltpu.VMEM)
    with jax.named_scope("plane"):
        arrived = lax.all_to_all(both, ("x", "ylo", "yhi"), 0, 0, tiled=True)
        by_level = pl.pallas_call(
            expand_kernel,
            out_shape=jax.ShapeDtypeStruct((16 * 24, EDGE), jnp.float32),
            in_specs=[whole],
            out_specs=whole,
            compiler_params=params(),
        )(arrived)
    with jax.named_scope("levels"):
        arrived = lax.all_to_all(by_level.reshape(16, 24, EDGE), "z", 0, 0, tiled=True)
        by_device = pl.pallas_call(
            spread_kernel,
            out_shape=jax.ShapeDtypeStruct((STRIPS, 16, EDGE), jnp.float32),
            in_specs=[whole],
            out_specs=whole,
            compiler_params=params(),
        )(arrived)
    with jax.named_scope("spread"):
        arrived = lax.all_to_all(by_device, ("core", "x", "ylo", "yhi"), 0, 0, tiled=True)
        schur, reduced = pl.pallas_call(
            functools.partial(
                finish_kernel,
                scale=order * math.sqrt(scenarios),
                root=math.sqrt(order * scenarios),
            ),
            out_shape=(
                jax.ShapeDtypeStruct(coupling.shape, jnp.float32),
                jax.ShapeDtypeStruct((8, EDGE), jnp.float32),
            ),
            in_specs=[whole] * 3,
            out_specs=(whole, whole),
            compiler_params=params(),
        )(arrived.reshape(STRIPS * 16, EDGE), coupling, rhs_first.reshape(8, EDGE))
    return (schur, reduced.reshape(-1))


def solution(mesh):
    fine = Mesh(mesh.devices.reshape(4, 2, 2, 2, 16), ("x", "ylo", "core", "yhi", "z"))
    scenario = ("x", "ylo", "core", "yhi", "z")
    placed = (
        P(scenario, None, None),
        P(scenario, None, None),
        P(scenario, None),
        P(scenario, None),
        P(("yhi", "z"), None),
        P(),
    )
    return jax.shard_map(
        on_device,
        mesh=fine,
        in_specs=placed,
        out_specs=(P(("yhi", "z"), None), P()),
        check_vma=False,
    )
```

```python
import functools
import math

import jax
import jax.numpy as jnp
from jax import lax
from jax.experimental import pallas as pl
from jax.experimental.pallas import tpu as pltpu
from jax.sharding import Mesh
from jax.sharding import PartitionSpec as P

EDGE = 128
BLOCKS = 8
STRIPS = 32
LEVELS = 16
KEPT = 5
PIECE = 152
GAP = 36
CHUNKS = 2


def gram_kernel(
    factor, border, marks, second, keep, send,
    f_buf, b_buf, r_buf, m_buf, linked, packed, carried, sems,
):
    order = f_buf.shape[0]
    rows = order // CHUNKS
    small = [
        pltpu.make_async_copy(marks, m_buf, sems.at[0]),
        pltpu.make_async_copy(second, r_buf, sems.at[1]),
        pltpu.make_async_copy(border.at[0], b_buf, sems.at[2]),
    ]
    parts = [pl.ds(k * rows, rows) for k in range(CHUNKS)]
    loads = [
        pltpu.make_async_copy(factor.at[0, part], f_buf.at[part], sems.at[3 + k])
        for k, part in enumerate(parts)
    ]
    for copy in small + loads:
        copy.start()
    for copy in small:
        copy.wait()
    mask = jnp.concatenate(
        [jnp.full((1, EDGE), m_buf[0, b].astype(jnp.float32)) for b in range(BLOCKS)], axis=1
    )
    second_row = r_buf[...].astype(jnp.float32)
    vector = jnp.zeros(carried.shape, jnp.float32)
    for copy, where in zip(loads, parts):
        copy.wait()
        part = f_buf[where, :]
        product = jnp.dot(part, b_buf[...], preferred_element_type=jnp.float32) * mask
        rounded = product.astype(jnp.bfloat16)
        linked[where, :] = rounded
        local = jnp.sum(part.astype(jnp.float32) * second_row, axis=1, keepdims=True)
        local = local.astype(jnp.bfloat16).astype(jnp.float32)
        vector = vector + jnp.sum(local * rounded.astype(jnp.float32), axis=0, keepdims=True)
    carried[...] = vector

    def place(i, j, value):
        d = (j - i) % BLOCKS
        if d == 5:
            i, d, value = j, 3, jnp.transpose(value)
        if d < 4 or (d == 4 and i < 4):
            for q in range(4):
                at = (4 * i + q) * GAP
                packed[d, at : at + STRIPS, :] = value[STRIPS * q : STRIPS * (q + 1)]

    wide = 2 * EDGE
    for a in range(4):
        left = linked[:, wide * a : wide * (a + 1)]
        count = 3 if a < 2 else 2
        spans = [(a, min(count, 4 - a))]
        if a + count > 4:
            spans.append((0, a + count - 4))
        for start, length in spans:
            block = lax.dot_general(
                left,
                linked[:, wide * start : wide * (start + length)],
                (((0,), (0,)), ((), ())),
                preferred_element_type=jnp.float32,
            )
            for i in range(2):
                for j in range(2 * length):
                    place(
                        2 * a + i,
                        2 * start + j,
                        block[EDGE * i : EDGE * (i + 1), EDGE * j : EDGE * (j + 1)],
                    )
    core = lax.axis_index("core")
    for out, side in ((keep, core), (send, 1 - core)):
        for j in range(LEVELS):
            for d in range(KEPT):
                height = STRIPS if d < 4 else LEVELS
                out[j, 32 * d : 32 * d + height, :] = packed[
                    d, pl.ds(side * LEVELS + j, height, stride=GAP), :
                ]
            where = pl.ds(pl.multiple_of((side * 4 + j // 4) * EDGE, EDGE), EDGE)
            out[j, 144:, :] = jnp.broadcast_to(carried[:, where], (8, EDGE))


def group_everywhere(row, group):
    lane = lax.broadcasted_iota(jnp.int32, row.shape, 1)
    only = jnp.where(lane // 32 == group, row, 0.0)
    only = only + pltpu.roll(only, 32, 1)
    return only + pltpu.roll(only, 64, 1)


def expand_kernel(arrived, out):
    total = arrived[0]
    for k in range(1, arrived.shape[0]):
        total = total + arrived[k]
    height = 16
    row = lax.broadcasted_iota(jnp.int32, (STRIPS, EDGE), 0)
    lane = lax.broadcasted_iota(jnp.int32, (STRIPS, EDGE), 1)
    apart = row % 4 - lane // 32

    def put(slot, value):
        out[pl.ds(slot, LEVELS, stride=height), :] = value

    for d in range(KEPT):
        if d < 4:
            given = total[32 * d : 32 * d + 32]
            put(8 + d, given[LEVELS:])
        else:
            given = total[32 * d : 32 * d + LEVELS]
            given = jnp.concatenate([given, given], axis=0)
        put(d, given[:LEVELS])
        if d == 0:
            continue
        turned = given
        for k in range(-3, 4):
            if k == 0:
                continue
            moved = pltpu.roll(pltpu.roll(given, k % STRIPS, 0), (-32 * k) % EDGE, 1)
            turned = jnp.where(apart == k, moved, turned)
        if d < 4:
            turned = pltpu.roll(turned, 4 * d, 0)
            put(8 - d, turned[:LEVELS])
            put(16 - d, turned[LEVELS:])
        else:
            own = lax.axis_index("ylo") * 2 + lax.axis_index("yhi")
            vector = group_everywhere(total[144:145], own)
            put(12, jnp.where(apart[:LEVELS] == 0, vector, turned[:LEVELS]))


def spread_kernel(arrived, out):
    total = arrived[0]
    for k in range(1, arrived.shape[0]):
        total = total + arrived[k]
    group = lax.axis_index("z") % 4
    lane = lax.broadcasted_iota(jnp.int32, (8, EDGE), 1)
    row = lax.broadcasted_iota(jnp.int32, (8, EDGE), 0)
    shared = jnp.broadcast_to(total[4:5], (8, EDGE))
    upper = jnp.where((row == 4) & (lane // 32 == group), shared, total[8:])
    vector = jnp.broadcast_to(group_everywhere(total[12:13], group), (8, EDGE))
    for j in range(STRIPS):
        out[j, :8, :] = upper if j % 2 else total[:8]
        out[j, 8:, :] = vector


def finish_kernel(arrived, coupling, first, schur, reduced, *, scale, root):
    high, z = lax.axis_index("yhi"), lax.axis_index("z")
    own = high * 4 + z // 4
    height = 16
    slots = [arrived[pl.ds(slot, STRIPS, stride=height), :] for slot in range(8)]
    flipped = jnp.transpose(jnp.concatenate(slots[4:], axis=0))
    for slot in range(8):
        value = slots[slot]
        if slot >= 4:
            at = (slot - 4) * STRIPS
            mirrored = jnp.concatenate(
                [flipped[32 * q : 32 * q + 32, at : at + STRIPS] for q in range(4)], axis=1
            )
            value = mirrored if slot > 4 else jnp.where(high == 0, value, mirrored)
        where = pl.ds(pl.multiple_of(lax.rem(own + slot, 8) * EDGE, EDGE), EDGE)
        schur[:, where] = coupling[:, where] - value / jnp.float32(scale)
    lane = lax.broadcasted_iota(jnp.int32, (8, EDGE), 1)
    vector = arrived[pl.ds(8, 8, stride=4 * height), :]
    for k in range(1, 4):
        group = arrived[pl.ds(k * height + 8, 8, stride=4 * height), :]
        vector = jnp.where(lane // 32 == k, group, vector)
    reduced[...] = first[...] - vector / jnp.float32(root)


def on_device(factors, border, pattern, rhs_second, coupling, rhs_first):
    _, order, width = factors.shape
    scenarios = 512
    params = functools.partial(pltpu.CompilerParams, vmem_limit_bytes=48 * 1024 * 1024)
    half = jax.ShapeDtypeStruct((LEVELS, PIECE, EDGE), jnp.float32)
    whole = pl.BlockSpec(memory_space=pltpu.VMEM)
    with jax.named_scope("gram"):
        operands = [
            pltpu.with_memory_space_constraint(x, pltpu.HBM)
            for x in (factors, border, pattern, rhs_second)
        ]
        keep, send = pl.pallas_call(
            gram_kernel,
            out_shape=(half, half),
            in_specs=[pl.BlockSpec(memory_space=pltpu.HBM)] * 4,
            out_specs=(whole, whole),
            scratch_shapes=[
                pltpu.VMEM((order, width), jnp.bfloat16),
                pltpu.VMEM((order, width), jnp.bfloat16),
                pltpu.VMEM((1, width), jnp.bfloat16),
                pltpu.SMEM((1, BLOCKS), jnp.int32),
                pltpu.VMEM((order, width), jnp.bfloat16),
                pltpu.VMEM((KEPT, STRIPS * GAP, EDGE), jnp.float32),
                pltpu.VMEM((1, width), jnp.float32),
                pltpu.SemaphoreType.DMA((3 + CHUNKS,)),
            ],
            compiler_params=params(),
        )(*operands)
    with jax.named_scope("cores"):
        both = keep + lax.ppermute(send, "core", [(0, 1), (1, 0)])
    with jax.named_scope("plane"):
        arrived = lax.all_to_all(both, ("x", "ylo", "yhi"), 0, 0, tiled=True)
        by_level = pl.pallas_call(
            expand_kernel,
            out_shape=jax.ShapeDtypeStruct((LEVELS * 16, EDGE), jnp.float32),
            in_specs=[whole],
            out_specs=whole,
            compiler_params=params(),
        )(arrived)
    with jax.named_scope("levels"):
        arrived = lax.all_to_all(by_level.reshape(LEVELS, 16, EDGE), "z", 0, 0, tiled=True)
        by_device = pl.pallas_call(
            spread_kernel,
            out_shape=jax.ShapeDtypeStruct((STRIPS, 16, EDGE), jnp.float32),
            in_specs=[whole],
            out_specs=whole,
            compiler_params=params(),
        )(arrived)
    with jax.named_scope("spread"):
        arrived = lax.all_to_all(by_device, ("core", "x", "ylo", "yhi"), 0, 0, tiled=True)
        schur, reduced = pl.pallas_call(
            functools.partial(
                finish_kernel,
                scale=order * math.sqrt(scenarios),
                root=math.sqrt(order * scenarios),
            ),
            out_shape=(
                jax.ShapeDtypeStruct(coupling.shape, jnp.float32),
                jax.ShapeDtypeStruct((8, EDGE), jnp.float32),
            ),
            in_specs=[whole] * 3,
            out_specs=(whole, whole),
            compiler_params=params(),
        )(arrived.reshape(STRIPS * 16, EDGE), coupling, rhs_first.reshape(8, EDGE))
    return (schur, reduced.reshape(-1))


def solution(mesh):
    fine = Mesh(mesh.devices.reshape(4, 2, 2, 2, 16), ("x", "ylo", "core", "yhi", "z"))
    scenario = ("x", "ylo", "core", "yhi", "z")
    placed = (
        P(scenario, None, None),
        P(scenario, None, None),
        P(scenario, None),
        P(scenario, None),
        P(("yhi", "z"), None),
        P(),
    )
    return jax.shard_map(
        on_device,
        mesh=fine,
        in_specs=placed,
        out_specs=(P(("yhi", "z"), None), P()),
        check_vma=False,
    )
```

```python
import functools
import math

import jax
import jax.numpy as jnp
from jax import lax
from jax.experimental import pallas as pl
from jax.experimental.pallas import tpu as pltpu
from jax.sharding import Mesh
from jax.sharding import PartitionSpec as P

EDGE = 128
BLOCKS = 8
STRIPS = 32
LEVELS = 16
KEPT = 5
PIECE = 136
START = (0, 24, 56, 88, 120)
COUNT = (20, 32, 32, 32, 16)
GAP = 36
CHUNKS = 2


def gram_kernel(
    factor, border, marks, second, keep, send,
    f_buf, b_buf, r_buf, m_buf, linked, packed, carried, sems,
):
    order = f_buf.shape[0]
    rows = order // CHUNKS
    small = [
        pltpu.make_async_copy(marks, m_buf, sems.at[0]),
        pltpu.make_async_copy(second, r_buf, sems.at[1]),
        pltpu.make_async_copy(border.at[0], b_buf, sems.at[2]),
    ]
    parts = [pl.ds(k * rows, rows) for k in range(CHUNKS)]
    loads = [
        pltpu.make_async_copy(factor.at[0, part], f_buf.at[part], sems.at[3 + k])
        for k, part in enumerate(parts)
    ]
    for copy in small + loads:
        copy.start()
    for copy in small:
        copy.wait()
    mask = jnp.concatenate(
        [jnp.full((1, EDGE), m_buf[0, b].astype(jnp.float32)) for b in range(BLOCKS)], axis=1
    )
    second_row = r_buf[...].astype(jnp.float32)
    vector = jnp.zeros(carried.shape, jnp.float32)
    for copy, where in zip(loads, parts):
        copy.wait()
        part = f_buf[where, :]
        product = jnp.dot(part, b_buf[...], preferred_element_type=jnp.float32) * mask
        rounded = product.astype(jnp.bfloat16)
        linked[where, :] = rounded
        local = jnp.sum(part.astype(jnp.float32) * second_row, axis=1, keepdims=True)
        local = local.astype(jnp.bfloat16).astype(jnp.float32)
        vector = vector + jnp.sum(local * rounded.astype(jnp.float32), axis=0, keepdims=True)
    carried[...] = vector

    lane = lax.broadcasted_iota(jnp.int32, (STRIPS, EDGE), 1)
    waiting = {}

    def place(i, j, value):
        d = (j - i) % BLOCKS
        if d == 0:
            strips = [value[STRIPS * q : STRIPS * (q + 1)] for q in range(4)]
            both = jnp.where(lane < 32, pltpu.roll(strips[3], 32, 1), strips[1])
            packed[0, i * GAP : i * GAP + STRIPS, :] = strips[0]
            packed[0, (8 + i) * GAP : (8 + i) * GAP + STRIPS, :] = both
            if i < 4:
                waiting[i] = strips[2]
            else:
                at = (12 + i) * GAP
                pair = jnp.where(lane < 64, pltpu.roll(strips[2], 64, 1), waiting[i - 4])
                packed[0, at : at + STRIPS, :] = pair
            return
        if d == 5:
            i, d, value = j, 3, jnp.transpose(value)
        if d < 4 or (d == 4 and i < 4):
            for q in range(4):
                at = (4 * i + q) * GAP
                packed[d, at : at + STRIPS, :] = value[STRIPS * q : STRIPS * (q + 1)]

    wide = 2 * EDGE
    for a in range(4):
        left = linked[:, wide * a : wide * (a + 1)]
        count = 3 if a < 2 else 2
        spans = [(a, min(count, 4 - a))]
        if a + count > 4:
            spans.append((0, a + count - 4))
        for start, length in spans:
            block = lax.dot_general(
                left,
                linked[:, wide * start : wide * (start + length)],
                (((0,), (0,)), ((), ())),
                preferred_element_type=jnp.float32,
            )
            for i in range(2):
                for j in range(2 * length):
                    place(
                        2 * a + i,
                        2 * start + j,
                        block[EDGE * i : EDGE * (i + 1), EDGE * j : EDGE * (j + 1)],
                    )
    core = lax.axis_index("core")
    for out, side in ((keep, core), (send, 1 - core)):
        for j in range(LEVELS):
            for d in range(KEPT):
                out[j, START[d] : START[d] + COUNT[d], :] = packed[
                    d, pl.ds(side * LEVELS + j, COUNT[d], stride=GAP), :
                ]
            where = pl.ds(pl.multiple_of((side * 4 + j // 4) * EDGE, EDGE), EDGE)
            out[j, 20:24, :] = jnp.broadcast_to(carried[:, where], (4, EDGE))


def group_everywhere(row, group):
    lane = lax.broadcasted_iota(jnp.int32, row.shape, 1)
    only = jnp.where(lane // 32 == group, row, 0.0)
    only = only + pltpu.roll(only, 32, 1)
    return only + pltpu.roll(only, 64, 1)


def expand_kernel(arrived, out, diagonal):
    total = arrived[0]
    for k in range(1, arrived.shape[0]):
        total = total + arrived[k]
    height = 16
    row = lax.broadcasted_iota(jnp.int32, (STRIPS, EDGE), 0)
    lane = lax.broadcasted_iota(jnp.int32, (STRIPS, EDGE), 1)
    apart = row % 4 - lane // 32

    def put(slot, value):
        out[pl.ds(slot, LEVELS, stride=height), :] = value

    mixed = total[8:16]
    diagonal[pl.ds(0, 8, stride=4), :] = total[:8]
    diagonal[pl.ds(1, 8, stride=4), :] = mixed
    diagonal[pl.ds(2, 8, stride=4), :] = jnp.concatenate(
        [total[16:20], pltpu.roll(total[16:20], 64, 1)], axis=0
    )
    diagonal[pl.ds(3, 8, stride=4), :] = pltpu.roll(mixed, 96, 1)
    for d in range(KEPT):
        if d == 0:
            given = diagonal[...]
        else:
            given = total[START[d] : START[d] + COUNT[d]]
        if d == KEPT - 1:
            given = jnp.concatenate([given, given], axis=0)
        turned = given
        for k in range(-3, 4):
            if k == 0:
                continue
            moved = pltpu.roll(pltpu.roll(given, k % STRIPS, 0), (-32 * k) % EDGE, 1)
            turned = jnp.where(apart == k, moved, turned)
        if d == 0:
            given = jnp.where(apart <= 0, given, turned)
        put(d, given[:LEVELS])
        if d < 4:
            put(8 + d, given[LEVELS:])
        if d == 0:
            continue
        if d < 4:
            turned = pltpu.roll(turned, 4 * d, 0)
            put(8 - d, turned[:LEVELS])
            put(16 - d, turned[LEVELS:])
        else:
            own = lax.axis_index("ylo") * 2 + lax.axis_index("yhi")
            vector = group_everywhere(total[20:21], own)
            put(12, jnp.where(apart[:LEVELS] == 0, vector, turned[:LEVELS]))


def spread_kernel(arrived, out):
    total = arrived[0]
    for k in range(1, arrived.shape[0]):
        total = total + arrived[k]
    group = lax.axis_index("z") % 4
    lane = lax.broadcasted_iota(jnp.int32, (8, EDGE), 1)
    row = lax.broadcasted_iota(jnp.int32, (8, EDGE), 0)
    shared = jnp.broadcast_to(total[4:5], (8, EDGE))
    upper = jnp.where((row == 4) & (lane // 32 == group), shared, total[8:])
    vector = group_everywhere(total[12:13], group)
    for j in range(STRIPS):
        strip = upper if j % 2 else total[:8]
        for slot in range(8):
            out[j, :, EDGE * slot : EDGE * (slot + 1)] = strip[slot : slot + 1]
        out[j, :, 8 * EDGE :] = vector


def finish_kernel(arrived, coupling, first, schur, reduced, *, scale, root):
    high, z = lax.axis_index("yhi"), lax.axis_index("z")
    own = high * 4 + z // 4
    slots = [arrived[:, 0, EDGE * slot : EDGE * (slot + 1)] for slot in range(8)]
    flipped = jnp.transpose(jnp.concatenate(slots[4:], axis=0))
    first_flipped = jnp.transpose(slots[0])
    lane = lax.broadcasted_iota(jnp.int32, (STRIPS, EDGE), 1)
    for slot in range(8):
        value = slots[slot]
        if slot == 0 or slot >= 4:
            source, at = (flipped, (slot - 4) * STRIPS) if slot else (first_flipped, 0)
            mirrored = jnp.concatenate(
                [source[32 * q : 32 * q + 32, at : at + STRIPS] for q in range(4)], axis=1
            )
            if slot == 0:
                value = jnp.where(lane // 32 >= z % 4, value, mirrored)
            elif slot == 4:
                value = jnp.where(high == 0, value, mirrored)
            else:
                value = mirrored
        where = pl.ds(pl.multiple_of(lax.rem(own + slot, 8) * EDGE, EDGE), EDGE)
        schur[:, where] = coupling[:, where] - value / jnp.float32(scale)
    lane = lax.broadcasted_iota(jnp.int32, (8, EDGE), 1)
    pieces = arrived[:, 0, 8 * EDGE :].reshape(8, 4, EDGE)
    vector = pieces[:, 0]
    for k in range(1, 4):
        vector = jnp.where(lane // 32 == k, pieces[:, k], vector)
    reduced[...] = first[...] - vector / jnp.float32(root)


def on_device(factors, border, pattern, rhs_second, coupling, rhs_first):
    _, order, width = factors.shape
    scenarios = 512
    params = functools.partial(pltpu.CompilerParams, vmem_limit_bytes=48 * 1024 * 1024)
    half = jax.ShapeDtypeStruct((LEVELS, PIECE, EDGE), jnp.float32)
    whole = pl.BlockSpec(memory_space=pltpu.VMEM)
    with jax.named_scope("gram"):
        operands = [
            pltpu.with_memory_space_constraint(x, pltpu.HBM)
            for x in (factors, border, pattern, rhs_second)
        ]
        keep, send = pl.pallas_call(
            gram_kernel,
            out_shape=(half, half),
            in_specs=[pl.BlockSpec(memory_space=pltpu.HBM)] * 4,
            out_specs=(whole, whole),
            scratch_shapes=[
                pltpu.VMEM((order, width), jnp.bfloat16),
                pltpu.VMEM((order, width), jnp.bfloat16),
                pltpu.VMEM((1, width), jnp.bfloat16),
                pltpu.SMEM((1, BLOCKS), jnp.int32),
                pltpu.VMEM((order, width), jnp.bfloat16),
                pltpu.VMEM((KEPT, STRIPS * GAP, EDGE), jnp.float32),
                pltpu.VMEM((1, width), jnp.float32),
                pltpu.SemaphoreType.DMA((3 + CHUNKS,)),
            ],
            compiler_params=params(),
        )(*operands)
    with jax.named_scope("cores"):
        both = keep + lax.ppermute(send, "core", [(0, 1), (1, 0)])
    with jax.named_scope("plane"):
        arrived = lax.all_to_all(both, ("x", "ylo", "yhi"), 0, 0, tiled=True)
        by_level = pl.pallas_call(
            expand_kernel,
            out_shape=jax.ShapeDtypeStruct((LEVELS * 16, EDGE), jnp.float32),
            in_specs=[whole],
            out_specs=whole,
            scratch_shapes=[pltpu.VMEM((STRIPS, EDGE), jnp.float32)],
            compiler_params=params(),
        )(arrived)
    with jax.named_scope("levels"):
        arrived = lax.all_to_all(by_level.reshape(LEVELS, 16, EDGE), "z", 0, 0, tiled=True)
        by_device = pl.pallas_call(
            spread_kernel,
            out_shape=jax.ShapeDtypeStruct((STRIPS, 1, 9 * EDGE), jnp.float32),
            in_specs=[whole],
            out_specs=whole,
            compiler_params=params(),
        )(arrived)
    with jax.named_scope("spread"):
        arrived = lax.all_to_all(by_device, ("core", "x", "ylo", "yhi"), 0, 0, tiled=True)
        schur, reduced = pl.pallas_call(
            functools.partial(
                finish_kernel,
                scale=order * math.sqrt(scenarios),
                root=math.sqrt(order * scenarios),
            ),
            out_shape=(
                jax.ShapeDtypeStruct(coupling.shape, jnp.float32),
                jax.ShapeDtypeStruct((8, EDGE), jnp.float32),
            ),
            in_specs=[whole] * 3,
            out_specs=(whole, whole),
            compiler_params=params(),
        )(arrived, coupling, rhs_first.reshape(8, EDGE))
    return (schur, reduced.reshape(-1))


def solution(mesh):
    fine = Mesh(mesh.devices.reshape(4, 2, 2, 2, 16), ("x", "ylo", "core", "yhi", "z"))
    scenario = ("x", "ylo", "core", "yhi", "z")
    placed = (
        P(scenario, None, None),
        P(scenario, None, None),
        P(scenario, None),
        P(scenario, None),
        P(("yhi", "z"), None),
        P(),
    )
    return jax.shard_map(
        on_device,
        mesh=fine,
        in_specs=placed,
        out_specs=(P(("yhi", "z"), None), P()),
        check_vma=False,
    )
```

```python
import functools
import math

import jax
import jax.numpy as jnp
from jax import lax
from jax.experimental import pallas as pl
from jax.experimental.pallas import tpu as pltpu
from jax.sharding import Mesh
from jax.sharding import PartitionSpec as P

EDGE = 128
BLOCKS = 8
STRIPS = 32
LEVELS = 16
KEPT = 5
PIECE = 136
START = (0, 24, 56, 88, 120)
COUNT = (20, 32, 32, 32, 16)
GAP = 36
CHUNKS = 2


AXES = ("x", "ylo", "core", "yhi", "z")


def place_of(x, y, core, z):
    return (((x * 2 + y % 2) * 2 + core) * 2 + y // 2) * 16 + z


ORDERS = (
    [(x, y) for x in range(4) for y in range(4)],
    [(3 - x, 3 - y) for y in range(4) for x in range(4)],
)
PIECES = [(x, y, core) for core in range(2) for x, y in ORDERS[core]]
PLANE = [[place_of(x, y, core, z) for x, y in ORDERS[core]] for core in range(2) for z in range(16)]
UPWARD = [
    [place_of(x, y, core, z if core == 0 else 15 - z) for z in range(16)]
    for x in range(4)
    for y in range(4)
    for core in range(2)
]
READERS = [(0, 2, 0), (2, 2, 0), (0, 0, 0), (3, 2, 0), (1, 2, 0), (1, 1, 0), (0, 3, 0), (2, 0, 0), (1, 3, 0), (2, 3, 0), (3, 3, 0), (0, 1, 0), (3, 0, 0), (3, 1, 0), (2, 1, 0), (1, 0, 0), (0, 2, 1), (0, 3, 1), (2, 3, 1), (2, 2, 1), (2, 0, 1), (0, 1, 1), (1, 1, 1), (1, 0, 1), (1, 3, 1), (3, 3, 1), (2, 1, 1), (3, 0, 1), (1, 2, 1), (3, 1, 1), (3, 2, 1), (0, 0, 1)]
SPREAD = [[place_of(x, y, core, z) for x, y, core in READERS] for z in range(16)]


def gram_kernel(
    factor, border, marks, second, keep, send,
    f_buf, b_buf, r_buf, m_buf, linked, packed, carried, sems,
):
    order = f_buf.shape[0]
    rows = order // CHUNKS
    small = [
        pltpu.make_async_copy(marks, m_buf, sems.at[0]),
        pltpu.make_async_copy(second, r_buf, sems.at[1]),
        pltpu.make_async_copy(border.at[0], b_buf, sems.at[2]),
    ]
    parts = [pl.ds(k * rows, rows) for k in range(CHUNKS)]
    loads = [
        pltpu.make_async_copy(factor.at[0, part], f_buf.at[part], sems.at[3 + k])
        for k, part in enumerate(parts)
    ]
    for copy in small + loads:
        copy.start()
    for copy in small:
        copy.wait()
    mask = jnp.concatenate(
        [jnp.full((1, EDGE), m_buf[0, b].astype(jnp.float32)) for b in range(BLOCKS)], axis=1
    )
    second_row = r_buf[...].astype(jnp.float32)
    vector = jnp.zeros(carried.shape, jnp.float32)
    for copy, where in zip(loads, parts):
        copy.wait()
        part = f_buf[where, :]
        product = jnp.dot(part, b_buf[...], preferred_element_type=jnp.float32) * mask
        rounded = product.astype(jnp.bfloat16)
        linked[where, :] = rounded
        local = jnp.sum(part.astype(jnp.float32) * second_row, axis=1, keepdims=True)
        local = local.astype(jnp.bfloat16).astype(jnp.float32)
        vector = vector + jnp.sum(local * rounded.astype(jnp.float32), axis=0, keepdims=True)
    carried[...] = vector

    lane = lax.broadcasted_iota(jnp.int32, (STRIPS, EDGE), 1)
    waiting = {}

    def place(i, j, value):
        d = (j - i) % BLOCKS
        if d == 0:
            strips = [value[STRIPS * q : STRIPS * (q + 1)] for q in range(4)]
            both = jnp.where(lane < 32, pltpu.roll(strips[3], 32, 1), strips[1])
            packed[0, i * GAP : i * GAP + STRIPS, :] = strips[0]
            packed[0, (8 + i) * GAP : (8 + i) * GAP + STRIPS, :] = both
            if i < 4:
                waiting[i] = strips[2]
            else:
                at = (12 + i) * GAP
                pair = jnp.where(lane < 64, pltpu.roll(strips[2], 64, 1), waiting[i - 4])
                packed[0, at : at + STRIPS, :] = pair
            return
        if d == 5:
            i, d, value = j, 3, jnp.transpose(value)
        if d < 4 or (d == 4 and i < 4):
            for q in range(4):
                at = (4 * i + q) * GAP
                packed[d, at : at + STRIPS, :] = value[STRIPS * q : STRIPS * (q + 1)]

    wide = 2 * EDGE
    for a in range(4):
        left = linked[:, wide * a : wide * (a + 1)]
        count = 3 if a < 2 else 2
        spans = [(a, min(count, 4 - a))]
        if a + count > 4:
            spans.append((0, a + count - 4))
        for start, length in spans:
            block = lax.dot_general(
                left,
                linked[:, wide * start : wide * (start + length)],
                (((0,), (0,)), ((), ())),
                preferred_element_type=jnp.float32,
            )
            for i in range(2):
                for j in range(2 * length):
                    place(
                        2 * a + i,
                        2 * start + j,
                        block[EDGE * i : EDGE * (i + 1), EDGE * j : EDGE * (j + 1)],
                    )
    core = lax.axis_index("core")
    for out, side in ((keep, core), (send, 1 - core)):
        for j in range(LEVELS):
            for d in range(KEPT):
                out[j, START[d] : START[d] + COUNT[d], :] = packed[
                    d, pl.ds(side * LEVELS + j, COUNT[d], stride=GAP), :
                ]
            where = pl.ds(pl.multiple_of((side * 4 + j // 4) * EDGE, EDGE), EDGE)
            out[j, 20:24, :] = jnp.broadcast_to(carried[:, where], (4, EDGE))


def group_everywhere(row, group):
    lane = lax.broadcasted_iota(jnp.int32, row.shape, 1)
    only = jnp.where(lane // 32 == group, row, 0.0)
    only = only + pltpu.roll(only, 32, 1)
    return only + pltpu.roll(only, 64, 1)


def expand_kernel(arrived, out, diagonal, by_z):
    total = arrived[0]
    for k in range(1, arrived.shape[0]):
        total = total + arrived[k]
    height = 16
    core = lax.axis_index("core")
    row = lax.broadcasted_iota(jnp.int32, (STRIPS, EDGE), 0)
    lane = lax.broadcasted_iota(jnp.int32, (STRIPS, EDGE), 1)
    apart = row % 4 - lane // 32

    def put(slot, value):
        by_z[pl.ds(slot, LEVELS, stride=height), :] = value

    mixed = total[8:16]
    diagonal[pl.ds(0, 8, stride=4), :] = total[:8]
    diagonal[pl.ds(1, 8, stride=4), :] = mixed
    diagonal[pl.ds(2, 8, stride=4), :] = jnp.concatenate(
        [total[16:20], pltpu.roll(total[16:20], 64, 1)], axis=0
    )
    diagonal[pl.ds(3, 8, stride=4), :] = pltpu.roll(mixed, 96, 1)
    for d in range(KEPT):
        if d == 0:
            given = diagonal[...]
        else:
            given = total[START[d] : START[d] + COUNT[d]]
        if d == KEPT - 1:
            given = jnp.concatenate([given, given], axis=0)
        turned = given
        for k in range(-3, 4):
            if k == 0:
                continue
            moved = pltpu.roll(pltpu.roll(given, k % STRIPS, 0), (-32 * k) % EDGE, 1)
            turned = jnp.where(apart == k, moved, turned)
        if d == 0:
            given = jnp.where(apart <= 0, given, turned)
        put(d, given[:LEVELS])
        if d < 4:
            put(8 + d, given[LEVELS:])
        if d == 0:
            continue
        if d < 4:
            turned = pltpu.roll(turned, 4 * d, 0)
            put(8 - d, turned[:LEVELS])
            put(16 - d, turned[LEVELS:])
        else:
            own = 0
            y = lax.axis_index("yhi") * 2 + lax.axis_index("ylo")
            chip = (lax.axis_index("x") * 4 + y) * 2 + core
            for p, (x, y, side) in enumerate(PIECES):
                own = own + jnp.where(chip == (x * 4 + y) * 2 + side, p % 4, 0)
            vector = group_everywhere(total[20:21], own)
            put(12, jnp.where(apart[:LEVELS] == 0, vector, turned[:LEVELS]))
    for z in range(LEVELS):
        at = jnp.where(core == 0, z, LEVELS - 1 - z) * height
        out[pl.ds(pl.multiple_of(at, height), height), :] = by_z[z * height : (z + 1) * height, :]


def spread_kernel(arrived, out):
    total = arrived[0]
    for k in range(1, arrived.shape[0]):
        total = total + arrived[k]
    group = lax.axis_index("z") % 4
    lane = lax.broadcasted_iota(jnp.int32, (8, EDGE), 1)
    row = lax.broadcasted_iota(jnp.int32, (8, EDGE), 0)
    shared = jnp.broadcast_to(total[4:5], (8, EDGE))
    upper = jnp.where((row == 4) & (lane // 32 == group), shared, total[8:])
    vector = group_everywhere(total[12:13], group)
    for j in range(STRIPS):
        strip = upper if READERS[j][1] // 2 else total[:8]
        for slot in range(8):
            out[j, :, EDGE * slot : EDGE * (slot + 1)] = strip[slot : slot + 1]
        out[j, :, 8 * EDGE :] = vector


def finish_kernel(arrived, coupling, first, schur, reduced, *, scale, root):
    high, z = lax.axis_index("yhi"), lax.axis_index("z")
    own = high * 4 + z // 4
    sender = [READERS.index(piece) for piece in PIECES]

    def gathered(slot, pieces):
        where = slice(EDGE * slot, EDGE * (slot + 1))
        return jnp.concatenate([arrived[sender[p], :, where] for p in pieces], axis=0)

    slots = [gathered(slot, range(STRIPS)) for slot in range(8)]
    flipped = jnp.transpose(jnp.concatenate(slots[4:], axis=0))
    first_flipped = jnp.transpose(slots[0])
    lane = lax.broadcasted_iota(jnp.int32, (STRIPS, EDGE), 1)
    for slot in range(8):
        value = slots[slot]
        if slot == 0 or slot >= 4:
            source, at = (flipped, (slot - 4) * STRIPS) if slot else (first_flipped, 0)
            mirrored = jnp.concatenate(
                [source[32 * q : 32 * q + 32, at : at + STRIPS] for q in range(4)], axis=1
            )
            if slot == 0:
                value = jnp.where(lane // 32 >= z % 4, value, mirrored)
            elif slot == 4:
                value = jnp.where(high == 0, value, mirrored)
            else:
                value = mirrored
        where = pl.ds(pl.multiple_of(lax.rem(own + slot, 8) * EDGE, EDGE), EDGE)
        schur[:, where] = coupling[:, where] - value / jnp.float32(scale)
    lane = lax.broadcasted_iota(jnp.int32, (8, EDGE), 1)
    vector = gathered(8, range(0, STRIPS, 4))
    for k in range(1, 4):
        vector = jnp.where(lane // 32 == k, gathered(8, range(k, STRIPS, 4)), vector)
    reduced[...] = first[...] - vector / jnp.float32(root)


def on_device(factors, border, pattern, rhs_second, coupling, rhs_first):
    _, order, width = factors.shape
    scenarios = 512
    params = functools.partial(pltpu.CompilerParams, vmem_limit_bytes=48 * 1024 * 1024)
    half = jax.ShapeDtypeStruct((LEVELS, PIECE, EDGE), jnp.float32)
    whole = pl.BlockSpec(memory_space=pltpu.VMEM)
    with jax.named_scope("gram"):
        operands = [
            pltpu.with_memory_space_constraint(x, pltpu.HBM)
            for x in (factors, border, pattern, rhs_second)
        ]
        keep, send = pl.pallas_call(
            gram_kernel,
            out_shape=(half, half),
            in_specs=[pl.BlockSpec(memory_space=pltpu.HBM)] * 4,
            out_specs=(whole, whole),
            scratch_shapes=[
                pltpu.VMEM((order, width), jnp.bfloat16),
                pltpu.VMEM((order, width), jnp.bfloat16),
                pltpu.VMEM((1, width), jnp.bfloat16),
                pltpu.SMEM((1, BLOCKS), jnp.int32),
                pltpu.VMEM((order, width), jnp.bfloat16),
                pltpu.VMEM((KEPT, STRIPS * GAP, EDGE), jnp.float32),
                pltpu.VMEM((1, width), jnp.float32),
                pltpu.SemaphoreType.DMA((3 + CHUNKS,)),
            ],
            compiler_params=params(),
        )(*operands)
    with jax.named_scope("cores"):
        both = keep + lax.ppermute(send, "core", [(0, 1), (1, 0)])
    with jax.named_scope("plane"):
        arrived = lax.all_to_all(both, AXES, 0, 0, axis_index_groups=PLANE, tiled=True)
        by_level = pl.pallas_call(
            expand_kernel,
            out_shape=jax.ShapeDtypeStruct((LEVELS * 16, EDGE), jnp.float32),
            in_specs=[whole],
            out_specs=whole,
            scratch_shapes=[
                pltpu.VMEM((STRIPS, EDGE), jnp.float32),
                pltpu.VMEM((LEVELS * 16, EDGE), jnp.float32),
            ],
            compiler_params=params(),
        )(arrived)
    with jax.named_scope("levels"):
        arrived = lax.all_to_all(
            by_level.reshape(LEVELS, 16, EDGE), AXES, 0, 0, axis_index_groups=UPWARD, tiled=True
        )
        by_device = pl.pallas_call(
            spread_kernel,
            out_shape=jax.ShapeDtypeStruct((STRIPS, 1, 9 * EDGE), jnp.float32),
            in_specs=[whole],
            out_specs=whole,
            compiler_params=params(),
        )(arrived)
    with jax.named_scope("spread"):
        arrived = lax.all_to_all(by_device, AXES, 0, 0, axis_index_groups=SPREAD, tiled=True)
        schur, reduced = pl.pallas_call(
            functools.partial(
                finish_kernel,
                scale=order * math.sqrt(scenarios),
                root=math.sqrt(order * scenarios),
            ),
            out_shape=(
                jax.ShapeDtypeStruct(coupling.shape, jnp.float32),
                jax.ShapeDtypeStruct((8, EDGE), jnp.float32),
            ),
            in_specs=[whole] * 3,
            out_specs=(whole, whole),
            compiler_params=params(),
        )(arrived, coupling, rhs_first.reshape(8, EDGE))
    return (schur, reduced.reshape(-1))


def solution(mesh):
    fine = Mesh(mesh.devices.reshape(4, 2, 2, 2, 16), ("x", "ylo", "core", "yhi", "z"))
    scenario = ("x", "ylo", "core", "yhi", "z")
    placed = (
        P(scenario, None, None),
        P(scenario, None, None),
        P(scenario, None),
        P(scenario, None),
        P(("yhi", "z"), None),
        P(),
    )
    return jax.shard_map(
        on_device,
        mesh=fine,
        in_specs=placed,
        out_specs=(P(("yhi", "z"), None), P()),
        check_vma=False,
    )
```

```python
import functools
import math

import jax
import jax.numpy as jnp
from jax import lax
from jax.experimental import pallas as pl
from jax.experimental.pallas import tpu as pltpu
from jax.sharding import Mesh
from jax.sharding import PartitionSpec as P

EDGE = 128
BLOCKS = 8
STRIPS = 32
LEVELS = 16
KEPT = 5
PIECE = 136
START = (0, 24, 56, 88, 120)
COUNT = (20, 32, 32, 32, 16)
GAP = 36
CHUNKS = 2


AXES = ("x", "ylo", "core", "yhi", "z")


def place_of(x, y, core, z):
    return (((x * 2 + y % 2) * 2 + core) * 2 + y // 2) * 16 + z


ORDERS = (
    [(x, y) for x in range(4) for y in range(4)],
    [(3 - x, 3 - y) for y in range(4) for x in range(4)],
)
PIECES = [(x, y, core) for core in range(2) for x, y in ORDERS[core]]
PLANE = [[place_of(x, y, core, z) for x, y in ORDERS[core]] for core in range(2) for z in range(16)]
LEVEL_ORDERS = (
    [4, 11, 10, 13, 12, 3, 6, 0, 1, 15, 14, 5, 2, 8, 9, 7],
    [11, 4, 5, 2, 3, 12, 9, 15, 14, 0, 1, 10, 13, 7, 6, 8],
)
UPWARD = [
    [place_of(x, y, core, z) for z in LEVEL_ORDERS[core]]
    for x in range(4)
    for y in range(4)
    for core in range(2)
]
READERS = [(3, 2, 1), (2, 1, 1), (2, 2, 0), (1, 2, 1), (0, 2, 0), (1, 2, 0), (2, 3, 1), (0, 3, 1), (2, 3, 0), (0, 0, 0), (1, 1, 0), (1, 1, 1), (1, 0, 0), (0, 0, 1), (0, 1, 0), (1, 0, 1), (3, 0, 1), (0, 1, 1), (2, 2, 1), (1, 3, 1), (3, 3, 1), (0, 2, 1), (0, 3, 0), (2, 1, 0), (2, 0, 0), (3, 1, 0), (1, 3, 0), (3, 0, 0), (3, 3, 0), (2, 0, 1), (3, 1, 1), (3, 2, 0)]
SPREAD = [[place_of(x, y, core, z) for x, y, core in READERS] for z in range(16)]


def gram_kernel(
    factor, border, marks, second, keep, send,
    f_buf, b_buf, r_buf, m_buf, linked, packed, carried, sems,
):
    order = f_buf.shape[0]
    rows = order // CHUNKS
    small = [
        pltpu.make_async_copy(marks, m_buf, sems.at[0]),
        pltpu.make_async_copy(second, r_buf, sems.at[1]),
        pltpu.make_async_copy(border.at[0], b_buf, sems.at[2]),
    ]
    parts = [pl.ds(k * rows, rows) for k in range(CHUNKS)]
    loads = [
        pltpu.make_async_copy(factor.at[0, part], f_buf.at[part], sems.at[3 + k])
        for k, part in enumerate(parts)
    ]
    for copy in small + loads:
        copy.start()
    for copy in small:
        copy.wait()
    mask = jnp.concatenate(
        [jnp.full((1, EDGE), m_buf[0, b].astype(jnp.float32)) for b in range(BLOCKS)], axis=1
    )
    second_row = r_buf[...].astype(jnp.float32)
    vector = jnp.zeros(carried.shape, jnp.float32)
    for copy, where in zip(loads, parts):
        copy.wait()
        part = f_buf[where, :]
        product = jnp.dot(part, b_buf[...], preferred_element_type=jnp.float32) * mask
        rounded = product.astype(jnp.bfloat16)
        linked[where, :] = rounded
        local = jnp.sum(part.astype(jnp.float32) * second_row, axis=1, keepdims=True)
        local = local.astype(jnp.bfloat16).astype(jnp.float32)
        vector = vector + jnp.sum(local * rounded.astype(jnp.float32), axis=0, keepdims=True)
    carried[...] = vector

    lane = lax.broadcasted_iota(jnp.int32, (STRIPS, EDGE), 1)
    waiting = {}

    def place(i, j, value):
        d = (j - i) % BLOCKS
        if d == 0:
            strips = [value[STRIPS * q : STRIPS * (q + 1)] for q in range(4)]
            both = jnp.where(lane < 32, pltpu.roll(strips[3], 32, 1), strips[1])
            packed[0, i * GAP : i * GAP + STRIPS, :] = strips[0]
            packed[0, (8 + i) * GAP : (8 + i) * GAP + STRIPS, :] = both
            if i < 4:
                waiting[i] = strips[2]
            else:
                at = (12 + i) * GAP
                pair = jnp.where(lane < 64, pltpu.roll(strips[2], 64, 1), waiting[i - 4])
                packed[0, at : at + STRIPS, :] = pair
            return
        if d == 5:
            i, d, value = j, 3, jnp.transpose(value)
        if d < 4 or (d == 4 and i < 4):
            for q in range(4):
                at = (4 * i + q) * GAP
                packed[d, at : at + STRIPS, :] = value[STRIPS * q : STRIPS * (q + 1)]

    wide = 2 * EDGE
    for a in range(4):
        left = linked[:, wide * a : wide * (a + 1)]
        count = 3 if a < 2 else 2
        spans = [(a, min(count, 4 - a))]
        if a + count > 4:
            spans.append((0, a + count - 4))
        for start, length in spans:
            block = lax.dot_general(
                left,
                linked[:, wide * start : wide * (start + length)],
                (((0,), (0,)), ((), ())),
                preferred_element_type=jnp.float32,
            )
            for i in range(2):
                for j in range(2 * length):
                    place(
                        2 * a + i,
                        2 * start + j,
                        block[EDGE * i : EDGE * (i + 1), EDGE * j : EDGE * (j + 1)],
                    )
    core = lax.axis_index("core")
    for out, side in ((keep, core), (send, 1 - core)):
        for j in range(LEVELS):
            for d in range(KEPT):
                out[j, START[d] : START[d] + COUNT[d], :] = packed[
                    d, pl.ds(side * LEVELS + j, COUNT[d], stride=GAP), :
                ]
            where = pl.ds(pl.multiple_of((side * 4 + j // 4) * EDGE, EDGE), EDGE)
            out[j, 20:24, :] = jnp.broadcast_to(carried[:, where], (4, EDGE))


def group_everywhere(row, group):
    lane = lax.broadcasted_iota(jnp.int32, row.shape, 1)
    only = jnp.where(lane // 32 == group, row, 0.0)
    only = only + pltpu.roll(only, 32, 1)
    return only + pltpu.roll(only, 64, 1)


def expand_kernel(arrived, out, diagonal, by_z):
    total = arrived[0]
    for k in range(1, arrived.shape[0]):
        total = total + arrived[k]
    height = 16
    core = lax.axis_index("core")
    row = lax.broadcasted_iota(jnp.int32, (STRIPS, EDGE), 0)
    lane = lax.broadcasted_iota(jnp.int32, (STRIPS, EDGE), 1)
    apart = row % 4 - lane // 32

    def put(slot, value):
        by_z[pl.ds(slot, LEVELS, stride=height), :] = value

    mixed = total[8:16]
    diagonal[pl.ds(0, 8, stride=4), :] = total[:8]
    diagonal[pl.ds(1, 8, stride=4), :] = mixed
    diagonal[pl.ds(2, 8, stride=4), :] = jnp.concatenate(
        [total[16:20], pltpu.roll(total[16:20], 64, 1)], axis=0
    )
    diagonal[pl.ds(3, 8, stride=4), :] = pltpu.roll(mixed, 96, 1)
    for d in range(KEPT):
        if d == 0:
            given = diagonal[...]
        else:
            given = total[START[d] : START[d] + COUNT[d]]
        if d == KEPT - 1:
            given = jnp.concatenate([given, given], axis=0)
        turned = given
        for k in range(-3, 4):
            if k == 0:
                continue
            moved = pltpu.roll(pltpu.roll(given, k % STRIPS, 0), (-32 * k) % EDGE, 1)
            turned = jnp.where(apart == k, moved, turned)
        if d == 0:
            given = jnp.where(apart <= 0, given, turned)
        put(d, given[:LEVELS])
        if d < 4:
            put(8 + d, given[LEVELS:])
        if d == 0:
            continue
        if d < 4:
            turned = pltpu.roll(turned, 4 * d, 0)
            put(8 - d, turned[:LEVELS])
            put(16 - d, turned[LEVELS:])
        else:
            own = 0
            y = lax.axis_index("yhi") * 2 + lax.axis_index("ylo")
            chip = (lax.axis_index("x") * 4 + y) * 2 + core
            for p, (x, y, side) in enumerate(PIECES):
                own = own + jnp.where(chip == (x * 4 + y) * 2 + side, p % 4, 0)
            vector = group_everywhere(total[20:21], own)
            put(12, jnp.where(apart[:LEVELS] == 0, vector, turned[:LEVELS]))
    for z in range(LEVELS):
        at = jnp.where(core == 0, LEVEL_ORDERS[0].index(z), LEVEL_ORDERS[1].index(z)) * height
        out[pl.ds(pl.multiple_of(at, height), height), :] = by_z[z * height : (z + 1) * height, :]


def spread_kernel(arrived, out):
    total = arrived[0]
    for k in range(1, arrived.shape[0]):
        total = total + arrived[k]
    group = lax.axis_index("z") % 4
    lane = lax.broadcasted_iota(jnp.int32, (8, EDGE), 1)
    row = lax.broadcasted_iota(jnp.int32, (8, EDGE), 0)
    shared = jnp.broadcast_to(total[4:5], (8, EDGE))
    upper = jnp.where((row == 4) & (lane // 32 == group), shared, total[8:])
    vector = group_everywhere(total[12:13], group)
    for j in range(STRIPS):
        strip = upper if READERS[j][1] // 2 else total[:8]
        for slot in range(8):
            out[j, :, EDGE * slot : EDGE * (slot + 1)] = strip[slot : slot + 1]
        out[j, :, 8 * EDGE :] = vector


def finish_kernel(arrived, coupling, first, schur, reduced, *, scale, root):
    high, z = lax.axis_index("yhi"), lax.axis_index("z")
    own = high * 4 + z // 4
    sender = [READERS.index(piece) for piece in PIECES]

    def gathered(slot, pieces):
        where = slice(EDGE * slot, EDGE * (slot + 1))
        return jnp.concatenate([arrived[sender[p], :, where] for p in pieces], axis=0)

    slots = [gathered(slot, range(STRIPS)) for slot in range(8)]
    flipped = jnp.transpose(jnp.concatenate(slots[4:], axis=0))
    first_flipped = jnp.transpose(slots[0])
    lane = lax.broadcasted_iota(jnp.int32, (STRIPS, EDGE), 1)
    for slot in range(8):
        value = slots[slot]
        if slot == 0 or slot >= 4:
            source, at = (flipped, (slot - 4) * STRIPS) if slot else (first_flipped, 0)
            mirrored = jnp.concatenate(
                [source[32 * q : 32 * q + 32, at : at + STRIPS] for q in range(4)], axis=1
            )
            if slot == 0:
                value = jnp.where(lane // 32 >= z % 4, value, mirrored)
            elif slot == 4:
                value = jnp.where(high == 0, value, mirrored)
            else:
                value = mirrored
        where = pl.ds(pl.multiple_of(lax.rem(own + slot, 8) * EDGE, EDGE), EDGE)
        schur[:, where] = coupling[:, where] - value / jnp.float32(scale)
    lane = lax.broadcasted_iota(jnp.int32, (8, EDGE), 1)
    vector = gathered(8, range(0, STRIPS, 4))
    for k in range(1, 4):
        vector = jnp.where(lane // 32 == k, gathered(8, range(k, STRIPS, 4)), vector)
    reduced[...] = first[...] - vector / jnp.float32(root)


def on_device(factors, border, pattern, rhs_second, coupling, rhs_first):
    _, order, width = factors.shape
    scenarios = 512
    params = functools.partial(pltpu.CompilerParams, vmem_limit_bytes=48 * 1024 * 1024)
    half = jax.ShapeDtypeStruct((LEVELS, PIECE, EDGE), jnp.float32)
    whole = pl.BlockSpec(memory_space=pltpu.VMEM)
    with jax.named_scope("gram"):
        operands = [
            pltpu.with_memory_space_constraint(x, pltpu.HBM)
            for x in (factors, border, pattern, rhs_second)
        ]
        keep, send = pl.pallas_call(
            gram_kernel,
            out_shape=(half, half),
            in_specs=[pl.BlockSpec(memory_space=pltpu.HBM)] * 4,
            out_specs=(whole, whole),
            scratch_shapes=[
                pltpu.VMEM((order, width), jnp.bfloat16),
                pltpu.VMEM((order, width), jnp.bfloat16),
                pltpu.VMEM((1, width), jnp.bfloat16),
                pltpu.SMEM((1, BLOCKS), jnp.int32),
                pltpu.VMEM((order, width), jnp.bfloat16),
                pltpu.VMEM((KEPT, STRIPS * GAP, EDGE), jnp.float32),
                pltpu.VMEM((1, width), jnp.float32),
                pltpu.SemaphoreType.DMA((3 + CHUNKS,)),
            ],
            compiler_params=params(),
        )(*operands)
    with jax.named_scope("cores"):
        both = keep + lax.ppermute(send, "core", [(0, 1), (1, 0)])
    with jax.named_scope("plane"):
        arrived = lax.all_to_all(both, AXES, 0, 0, axis_index_groups=PLANE, tiled=True)
        by_level = pl.pallas_call(
            expand_kernel,
            out_shape=jax.ShapeDtypeStruct((LEVELS * 16, EDGE), jnp.float32),
            in_specs=[whole],
            out_specs=whole,
            scratch_shapes=[
                pltpu.VMEM((STRIPS, EDGE), jnp.float32),
                pltpu.VMEM((LEVELS * 16, EDGE), jnp.float32),
            ],
            compiler_params=params(),
        )(arrived)
    with jax.named_scope("levels"):
        arrived = lax.all_to_all(
            by_level.reshape(LEVELS, 16, EDGE), AXES, 0, 0, axis_index_groups=UPWARD, tiled=True
        )
        by_device = pl.pallas_call(
            spread_kernel,
            out_shape=jax.ShapeDtypeStruct((STRIPS, 1, 9 * EDGE), jnp.float32),
            in_specs=[whole],
            out_specs=whole,
            compiler_params=params(),
        )(arrived)
    with jax.named_scope("spread"):
        arrived = lax.all_to_all(by_device, AXES, 0, 0, axis_index_groups=SPREAD, tiled=True)
        schur, reduced = pl.pallas_call(
            functools.partial(
                finish_kernel,
                scale=order * math.sqrt(scenarios),
                root=math.sqrt(order * scenarios),
            ),
            out_shape=(
                jax.ShapeDtypeStruct(coupling.shape, jnp.float32),
                jax.ShapeDtypeStruct((8, EDGE), jnp.float32),
            ),
            in_specs=[whole] * 3,
            out_specs=(whole, whole),
            compiler_params=params(),
        )(arrived, coupling, rhs_first.reshape(8, EDGE))
    return (schur, reduced.reshape(-1))


def solution(mesh):
    fine = Mesh(mesh.devices.reshape(4, 2, 2, 2, 16), ("x", "ylo", "core", "yhi", "z"))
    scenario = ("x", "ylo", "core", "yhi", "z")
    placed = (
        P(scenario, None, None),
        P(scenario, None, None),
        P(scenario, None),
        P(scenario, None),
        P(("yhi", "z"), None),
        P(),
    )
    return jax.shard_map(
        on_device,
        mesh=fine,
        in_specs=placed,
        out_specs=(P(("yhi", "z"), None), P()),
        check_vma=False,
    )
```

```python
import functools
import math

import jax
import jax.numpy as jnp
from jax import lax
from jax.experimental import pallas as pl
from jax.experimental.pallas import tpu as pltpu
from jax.sharding import Mesh
from jax.sharding import PartitionSpec as P

EDGE = 128
BLOCKS = 8
STRIPS = 32
LEVELS = 16
KEPT = 5
PIECE = 136
START = (0, 24, 56, 88, 120)
COUNT = (20, 32, 32, 32, 16)
GAP = 36
CHUNKS = 2


AXES = ("x", "ylo", "core", "yhi", "z")


def place_of(x, y, core, z):
    return (((x * 2 + y % 2) * 2 + core) * 2 + y // 2) * 16 + z


ORDERS = (
    [(x, y) for x in range(4) for y in range(4)],
    [(3 - x, 3 - y) for y in range(4) for x in range(4)],
)
PIECES = [(x, y, core) for core in range(2) for x, y in ORDERS[core]]
PLANE = [[place_of(x, y, core, z) for x, y in ORDERS[core]] for core in range(2) for z in range(16)]
LEVEL_ORDERS = (
    [4, 11, 10, 13, 12, 3, 6, 0, 1, 15, 14, 5, 2, 8, 9, 7],
    [11, 4, 5, 2, 3, 12, 9, 15, 14, 0, 1, 10, 13, 7, 6, 8],
)
UPWARD = [
    [place_of(x, y, core, z) for z in LEVEL_ORDERS[core]]
    for x in range(4)
    for y in range(4)
    for core in range(2)
]
READERS = [(3, 3, 0), (0, 0, 1), (0, 2, 1), (2, 2, 1), (1, 3, 0), (3, 0, 0), (1, 2, 0), (1, 1, 1), (3, 1, 1), (2, 3, 1), (3, 0, 1), (0, 1, 0), (2, 2, 0), (1, 2, 1), (2, 1, 0), (1, 0, 0), (0, 0, 0), (3, 3, 1), (2, 3, 0), (0, 2, 0), (3, 2, 0), (2, 1, 1), (2, 0, 1), (1, 3, 1), (1, 0, 1), (0, 1, 1), (3, 1, 0), (3, 2, 1), (0, 3, 1), (0, 3, 0), (1, 1, 0), (2, 0, 0)]
SPREAD = [[place_of(x, y, core, z) for x, y, core in READERS] for z in range(16)]


def gram_kernel(
    factor, border, marks, second, keep, send,
    f_buf, b_buf, r_buf, m_buf, linked, packed, carried, sems,
):
    order = f_buf.shape[0]
    rows = order // CHUNKS
    small = [
        pltpu.make_async_copy(marks, m_buf, sems.at[0]),
        pltpu.make_async_copy(second, r_buf, sems.at[1]),
        pltpu.make_async_copy(border.at[0], b_buf, sems.at[2]),
    ]
    parts = [pl.ds(k * rows, rows) for k in range(CHUNKS)]
    loads = [
        pltpu.make_async_copy(factor.at[0, part], f_buf.at[part], sems.at[3 + k])
        for k, part in enumerate(parts)
    ]
    for copy in small + loads:
        copy.start()
    for copy in small:
        copy.wait()
    mask = jnp.concatenate(
        [jnp.full((1, EDGE), m_buf[0, b].astype(jnp.float32)) for b in range(BLOCKS)], axis=1
    )
    second_row = r_buf[...].astype(jnp.float32)
    vector = jnp.zeros(carried.shape, jnp.float32)
    for copy, where in zip(loads, parts):
        copy.wait()
        part = f_buf[where, :]
        product = jnp.dot(part, b_buf[...], preferred_element_type=jnp.float32) * mask
        rounded = product.astype(jnp.bfloat16)
        linked[where, :] = rounded
        local = jnp.sum(part.astype(jnp.float32) * second_row, axis=1, keepdims=True)
        local = local.astype(jnp.bfloat16).astype(jnp.float32)
        vector = vector + jnp.sum(local * rounded.astype(jnp.float32), axis=0, keepdims=True)
    carried[...] = vector

    lane = lax.broadcasted_iota(jnp.int32, (STRIPS, EDGE), 1)
    waiting = {}

    def place(i, j, value):
        d = (j - i) % BLOCKS
        if d == 0:
            strips = [value[STRIPS * q : STRIPS * (q + 1)] for q in range(4)]
            both = jnp.where(lane < 32, pltpu.roll(strips[3], 32, 1), strips[1])
            packed[0, i * GAP : i * GAP + STRIPS, :] = strips[0]
            packed[0, (8 + i) * GAP : (8 + i) * GAP + STRIPS, :] = both
            if i < 4:
                waiting[i] = strips[2]
            else:
                at = (12 + i) * GAP
                pair = jnp.where(lane < 64, pltpu.roll(strips[2], 64, 1), waiting[i - 4])
                packed[0, at : at + STRIPS, :] = pair
            return
        if d == 5:
            i, d, value = j, 3, jnp.transpose(value)
        if d < 4 or (d == 4 and i < 4):
            for q in range(4):
                at = (4 * i + q) * GAP
                packed[d, at : at + STRIPS, :] = value[STRIPS * q : STRIPS * (q + 1)]

    wide = 2 * EDGE
    for a in range(4):
        left = linked[:, wide * a : wide * (a + 1)]
        count = 3 if a < 2 else 2
        spans = [(a, min(count, 4 - a))]
        if a + count > 4:
            spans.append((0, a + count - 4))
        for start, length in spans:
            block = lax.dot_general(
                left,
                linked[:, wide * start : wide * (start + length)],
                (((0,), (0,)), ((), ())),
                preferred_element_type=jnp.float32,
            )
            for i in range(2):
                for j in range(2 * length):
                    place(
                        2 * a + i,
                        2 * start + j,
                        block[EDGE * i : EDGE * (i + 1), EDGE * j : EDGE * (j + 1)],
                    )
    core = lax.axis_index("core")
    for out, side in ((keep, core), (send, 1 - core)):
        for j in range(LEVELS):
            for d in range(KEPT):
                out[j, START[d] : START[d] + COUNT[d], :] = packed[
                    d, pl.ds(side * LEVELS + j, COUNT[d], stride=GAP), :
                ]
            where = pl.ds(pl.multiple_of((side * 4 + j // 4) * EDGE, EDGE), EDGE)
            out[j, 20:24, :] = jnp.broadcast_to(carried[:, where], (4, EDGE))


def group_everywhere(row, group):
    lane = lax.broadcasted_iota(jnp.int32, row.shape, 1)
    only = jnp.where(lane // 32 == group, row, 0.0)
    only = only + pltpu.roll(only, 32, 1)
    return only + pltpu.roll(only, 64, 1)


def expand_kernel(arrived, out, diagonal, by_z):
    total = arrived[0]
    for k in range(1, arrived.shape[0]):
        total = total + arrived[k]
    height = 16
    core = lax.axis_index("core")
    row = lax.broadcasted_iota(jnp.int32, (STRIPS, EDGE), 0)
    lane = lax.broadcasted_iota(jnp.int32, (STRIPS, EDGE), 1)
    apart = row % 4 - lane // 32

    def put(slot, value):
        by_z[pl.ds(slot, LEVELS, stride=height), :] = value

    mixed = total[8:16]
    diagonal[pl.ds(0, 8, stride=4), :] = total[:8]
    diagonal[pl.ds(1, 8, stride=4), :] = mixed
    diagonal[pl.ds(2, 8, stride=4), :] = jnp.concatenate(
        [total[16:20], pltpu.roll(total[16:20], 64, 1)], axis=0
    )
    diagonal[pl.ds(3, 8, stride=4), :] = pltpu.roll(mixed, 96, 1)
    for d in range(KEPT):
        if d == 0:
            given = diagonal[...]
        else:
            given = total[START[d] : START[d] + COUNT[d]]
        if d == KEPT - 1:
            given = jnp.concatenate([given, given], axis=0)
        turned = given
        for k in range(-3, 4):
            if k == 0:
                continue
            moved = pltpu.roll(pltpu.roll(given, k % STRIPS, 0), (-32 * k) % EDGE, 1)
            turned = jnp.where(apart == k, moved, turned)
        if d == 0:
            given = jnp.where(apart <= 0, given, turned)
        put(d, given[:LEVELS])
        if d < 4:
            put(8 + d, given[LEVELS:])
        if d == 0:
            continue
        if d < 4:
            turned = pltpu.roll(turned, 4 * d, 0)
            put(8 - d, turned[:LEVELS])
            put(16 - d, turned[LEVELS:])
        else:
            own = 0
            y = lax.axis_index("yhi") * 2 + lax.axis_index("ylo")
            chip = (lax.axis_index("x") * 4 + y) * 2 + core
            for p, (x, y, side) in enumerate(PIECES):
                own = own + jnp.where(chip == (x * 4 + y) * 2 + side, p % 4, 0)
            vector = group_everywhere(total[20:21], own)
            put(12, jnp.where(apart[:LEVELS] == 0, vector, turned[:LEVELS]))
    for z in range(LEVELS):
        at = jnp.where(core == 0, LEVEL_ORDERS[0].index(z), LEVEL_ORDERS[1].index(z)) * height
        out[pl.ds(pl.multiple_of(at, height), height), :] = by_z[z * height : (z + 1) * height, :]


def spread_kernel(arrived, out):
    total = arrived[0]
    for k in range(1, arrived.shape[0]):
        total = total + arrived[k]
    group = lax.axis_index("z") % 4
    lane = lax.broadcasted_iota(jnp.int32, (8, EDGE), 1)
    row = lax.broadcasted_iota(jnp.int32, (8, EDGE), 0)
    shared = jnp.broadcast_to(total[4:5], (8, EDGE))
    upper = jnp.where((row == 4) & (lane // 32 == group), shared, total[8:])
    vector = group_everywhere(total[12:13], group)
    for j in range(STRIPS):
        strip = upper if READERS[j][1] // 2 else total[:8]
        for slot in range(8):
            out[j, :, EDGE * slot : EDGE * (slot + 1)] = strip[slot : slot + 1]
        out[j, :, 8 * EDGE :] = vector


def finish_kernel(arrived, coupling, first, schur, reduced, *, scale, root):
    high, z = lax.axis_index("yhi"), lax.axis_index("z")
    own = high * 4 + z // 4
    sender = [READERS.index(piece) for piece in PIECES]

    def gathered(slot, pieces):
        where = slice(EDGE * slot, EDGE * (slot + 1))
        return jnp.concatenate([arrived[sender[p], :, where] for p in pieces], axis=0)

    slots = [gathered(slot, range(STRIPS)) for slot in range(8)]
    flipped = jnp.transpose(jnp.concatenate(slots[4:], axis=0))
    first_flipped = jnp.transpose(slots[0])
    lane = lax.broadcasted_iota(jnp.int32, (STRIPS, EDGE), 1)
    for slot in range(8):
        value = slots[slot]
        if slot == 0 or slot >= 4:
            source, at = (flipped, (slot - 4) * STRIPS) if slot else (first_flipped, 0)
            mirrored = jnp.concatenate(
                [source[32 * q : 32 * q + 32, at : at + STRIPS] for q in range(4)], axis=1
            )
            if slot == 0:
                value = jnp.where(lane // 32 >= z % 4, value, mirrored)
            elif slot == 4:
                value = jnp.where(high == 0, value, mirrored)
            else:
                value = mirrored
        where = pl.ds(pl.multiple_of(lax.rem(own + slot, 8) * EDGE, EDGE), EDGE)
        schur[:, where] = coupling[:, where] - value / jnp.float32(scale)
    lane = lax.broadcasted_iota(jnp.int32, (8, EDGE), 1)
    vector = gathered(8, range(0, STRIPS, 4))
    for k in range(1, 4):
        vector = jnp.where(lane // 32 == k, gathered(8, range(k, STRIPS, 4)), vector)
    reduced[...] = first[...] - vector / jnp.float32(root)


def on_device(factors, border, pattern, rhs_second, coupling, rhs_first):
    _, order, width = factors.shape
    scenarios = 512
    params = functools.partial(pltpu.CompilerParams, vmem_limit_bytes=48 * 1024 * 1024)
    half = jax.ShapeDtypeStruct((LEVELS, PIECE, EDGE), jnp.float32)
    whole = pl.BlockSpec(memory_space=pltpu.VMEM)
    with jax.named_scope("gram"):
        operands = [
            pltpu.with_memory_space_constraint(x, pltpu.HBM)
            for x in (factors, border, pattern, rhs_second)
        ]
        keep, send = pl.pallas_call(
            gram_kernel,
            out_shape=(half, half),
            in_specs=[pl.BlockSpec(memory_space=pltpu.HBM)] * 4,
            out_specs=(whole, whole),
            scratch_shapes=[
                pltpu.VMEM((order, width), jnp.bfloat16),
                pltpu.VMEM((order, width), jnp.bfloat16),
                pltpu.VMEM((1, width), jnp.bfloat16),
                pltpu.SMEM((1, BLOCKS), jnp.int32),
                pltpu.VMEM((order, width), jnp.bfloat16),
                pltpu.VMEM((KEPT, STRIPS * GAP, EDGE), jnp.float32),
                pltpu.VMEM((1, width), jnp.float32),
                pltpu.SemaphoreType.DMA((3 + CHUNKS,)),
            ],
            compiler_params=params(),
        )(*operands)
    with jax.named_scope("cores"):
        both = keep + lax.ppermute(send, "core", [(0, 1), (1, 0)])
    with jax.named_scope("plane"):
        arrived = lax.all_to_all(both, AXES, 0, 0, axis_index_groups=PLANE, tiled=True)
        by_level = pl.pallas_call(
            expand_kernel,
            out_shape=jax.ShapeDtypeStruct((LEVELS * 16, EDGE), jnp.float32),
            in_specs=[whole],
            out_specs=whole,
            scratch_shapes=[
                pltpu.VMEM((STRIPS, EDGE), jnp.float32),
                pltpu.VMEM((LEVELS * 16, EDGE), jnp.float32),
            ],
            compiler_params=params(),
        )(arrived)
    with jax.named_scope("levels"):
        arrived = lax.all_to_all(
            by_level.reshape(LEVELS, 16, EDGE), AXES, 0, 0, axis_index_groups=UPWARD, tiled=True
        )
        by_device = pl.pallas_call(
            spread_kernel,
            out_shape=jax.ShapeDtypeStruct((STRIPS, 1, 9 * EDGE), jnp.float32),
            in_specs=[whole],
            out_specs=whole,
            compiler_params=params(),
        )(arrived)
    with jax.named_scope("spread"):
        arrived = lax.all_to_all(by_device, AXES, 0, 0, axis_index_groups=SPREAD, tiled=True)
        schur, reduced = pl.pallas_call(
            functools.partial(
                finish_kernel,
                scale=order * math.sqrt(scenarios),
                root=math.sqrt(order * scenarios),
            ),
            out_shape=(
                jax.ShapeDtypeStruct(coupling.shape, jnp.float32),
                jax.ShapeDtypeStruct((8, EDGE), jnp.float32),
            ),
            in_specs=[whole] * 3,
            out_specs=(whole, whole),
            compiler_params=params(),
        )(arrived, coupling, rhs_first.reshape(8, EDGE))
    return (schur, reduced.reshape(-1))


def solution(mesh):
    fine = Mesh(mesh.devices.reshape(4, 2, 2, 2, 16), ("x", "ylo", "core", "yhi", "z"))
    scenario = ("x", "ylo", "core", "yhi", "z")
    placed = (
        P(scenario, None, None),
        P(scenario, None, None),
        P(scenario, None),
        P(scenario, None),
        P(("yhi", "z"), None),
        P(),
    )
    return jax.shard_map(
        on_device,
        mesh=fine,
        in_specs=placed,
        out_specs=(P(("yhi", "z"), None), P()),
        check_vma=False,
    )
```
